32 devices in a mesh: dp: 8 (over z, x), tensor: 4 (over y, core).
Axes of the slice: x: 2, y: 2, z: 4, core: 2. Of those that a mesh axis runs over, the one named last changes fastest.
Arguments:
- hidden: bfloat16 [2048, 8192], P('dp', 'tensor'), may hold values from -6 to 6
- connector: bfloat16 [8192, 3584], P('tensor'), may hold values from -0.0625 to 0.0625
- routing: int32 [2048, 1], P('dp'), may hold values from 0 to 3; in each aligned block of 256 rows (0 to 255, 256 to 511, ...) at most 128 rows name the same one
- talker_in: bfloat16 [4096, 3584], P(('dp', 'tensor')), may hold values from -6 to 6
- norm_gain: float32 [3584], replicated, may hold values from 0.25 to 1.75
- kv_weight: bfloat16 [3584, 1024], replicated, may hold values from -0.09375 to 0.09375
- kv_grad: bfloat16 [4096, 1024], P(('dp', 'tensor')), may hold values from -6 to 6
Outputs:
- hidden_grad: bfloat16 [2048, 8192], P('dp', 'tensor')
- connector_grad: float32 [8192, 3584], P('tensor', 'dp')
- kv_weight_grad: float32 [3584, 1024], P(None, ('dp', 'tensor'))
The draws below stay inside these ranges and needn't reach their ends.
Inputs may be any that keep to these rules, and one draw needn't show every extreme that they name: `routing`: among the 256 rows of one index of dp, at most 128 go to one shard.
All inputs are finite; a program needn't handle non-finite values.
Results may differ from the reference program's by a relative error of at most 0.005.
Values may be sent and summed in bfloat16 or wider, within the bound.
No kernel may reach another device: no remote copies, remote signals or barrier semaphores. Data moves between devices by JAX's collectives and lax.ppermute only.
A program may use at most 128 MiB of HBM per device.

```python
import math
import jax
import jax.numpy as jnp
import numpy as np
from jax import lax

D = 8192
DT = 3584
KVW = 1024
TOK_DEV = 256
CAP = 128
TOKENS = 2048
SLOTS = 4096
N_DP = 8
N_TENSOR = 4


def raised(result, key, source, target, parts, factor):
    owner, partner = [(jnp.arange(result.shape[position]) // (result.shape[position] // parts)).reshape([-1 if axis == position else 1 for axis in range(result.ndim)]) for position in (source, target)]
    chosen = jax.random.permutation(key, parts)[partner]
    strong = (owner == chosen) | (owner == (partner + parts // 2) % parts)
    return jnp.where(strong, factor * result, result)


def shard_levels(stream_key, dims, split, low, high):
    level = 1.0
    for dim, blocks in split:
        heights = jax.random.uniform(jax.random.fold_in(jax.random.fold_in(stream_key, 6), dim), (blocks,), jnp.float32, low / len(split), high / len(split))
        level = level * jnp.repeat(jnp.exp(heights), dims[dim] // blocks).reshape((-1,) + (1,) * (len(dims) - 1 - dim))
    return level


def assign_block(key, own, number, rows, count, top, most, slope):
    order = jax.random.permutation(key, count)
    heavy_load, ordinary = shares(count, rows * top, most, slope, True), shares(count, rows * top, most, slope, False)
    places = jnp.arange(count)

    def named(lengths, turn):
        used = int((lengths > 0).sum())
        fixed = max(1, used // 4)
        shifted = fixed + (places - fixed + turn * (used - fixed)) % max(1, count - fixed)
        return jnp.zeros((count,), jnp.int32).at[order[jnp.where(places < fixed, places, shifted)]].set(jnp.asarray(lengths, jnp.int32))

    lengths = jnp.where(number % 4 == 0, named(heavy_load, number // 4), named(ordinary, number - number // 4 - 1))
    mixed = jax.random.permutation(jax.random.fold_in(own, 3), count)
    giver, receiver = mixed[0:count // 2 * 2:2], mixed[1:count // 2 * 2:2]
    slack = jnp.minimum(lengths[giver] - 1, most - lengths[receiver]) // 2
    slack = jnp.where((giver == order[0]) | (receiver == order[0]) | (lengths[receiver] == 0), 0, jnp.maximum(slack, 0))
    shifted = jax.random.randint(jax.random.fold_in(own, 4), (count // 2,), 0, 1 << 20) % (slack + 1)
    lengths = lengths.at[giver].add(-shifted).at[receiver].add(shifted)
    items = jnp.searchsorted(jnp.cumsum(lengths), jnp.arange(rows * top), side="right").astype(jnp.int32)
    listing = items.reshape(top, rows).T
    listing = listing[jax.random.permutation(jax.random.fold_in(own, 1), rows)]
    turn = jax.random.randint(jax.random.fold_in(own, 2), (rows, 1), 0, top)
    return jnp.take_along_axis(listing, (jnp.arange(top)[None, :] + turn) % top, axis=1)


def shares(amount, total, reach, lean, full):
    loads = [(1 << 20) // math.isqrt(standing ** lean) + 1 for standing in range(1, amount + 1)]
    largest = reach if full else min(reach, max(-(-total // amount), total * loads[0] // sum(loads)))
    least = 1 if total - largest >= amount - 1 else 0
    holding, rest = [largest] + [least] * (amount - 1), total - largest - least * (amount - 1)
    while rest > 0:
        free = [i for i in range(1, amount) if holding[i] < largest] or [i for i in range(1, amount) if holding[i] < reach]
        whole, budget = sum([loads[i] for i in free]), rest
        for i in free:
            extra = min(reach - holding[i], max(1, budget * loads[i] // whole), rest)
            holding[i] = holding[i] + extra
            rest = rest - extra
    return np.array(holding)


def bell_draw(stream_key, shape, scale, limit, split=(), kind=jnp.bfloat16):
    values = scale * jax.random.normal(stream_key, shape, jnp.float32)
    if split:
        values = values * shard_levels(stream_key, shape, split, -0.22, 0.18)
    return jnp.clip(values, -limit, limit).astype(kind)


def bell_draw_with(stream_key, extent, spread, most, cuts, heavy, kind=jnp.bfloat16):
    result = spread * jax.random.normal(stream_key, extent, jnp.float32)
    if cuts:
        result = result * shard_levels(stream_key, extent, cuts, -0.22, 0.18)
    return jnp.clip(raised(result, jax.random.fold_in(stream_key, 3), *heavy), -most, most).astype(kind)


def setup_inputs(seed: int = 0) -> dict:
    keys = jax.random.split(jax.random.key(seed), 8)
    hidden = bell_draw(keys[0], (TOKENS, D), 1.0, 6.0, ((0, 8), (1, 4)))
    connector = bell_draw(keys[1], (D, DT), D ** -0.5, 0.0625, ((0, 4),))
    routing_keys = jax.random.split(jax.random.fold_in(keys[2], 1), TOKENS // TOK_DEV)
    routing_turns = jax.random.permutation(jax.random.fold_in(keys[2], 3), TOKENS // TOK_DEV)
    routing = jax.vmap(lambda own, number: assign_block(jax.random.fold_in(keys[2], 2), own, number, TOK_DEV, N_TENSOR, 1, CAP, 1))(routing_keys, routing_turns).reshape((TOKENS, 1))
    talker_in = bell_draw(keys[3], (SLOTS, DT), 1.0, 6.0, ((0, 32),))
    norm_gain = jnp.clip(1.0 + 0.15 * jax.random.normal(keys[4], (DT,), jnp.float32), 0.25, 1.75)
    kv_weight = bell_draw(keys[5], (DT, KVW), DT ** -0.5, 0.09375)
    kv_grad = bell_draw_with(keys[6], (SLOTS, KVW), 1.0, 6.0, ((0, 32),), (0, 1, 32, 2.75))
    return {"hidden": hidden, "connector": connector, "routing": routing, "talker_in": talker_in, "norm_gain": norm_gain, "kv_weight": kv_weight, "kv_grad": kv_grad}


def slot_index(group_routes):
    shards = jnp.arange(N_TENSOR, dtype=jnp.int32)
    onehot = (group_routes[:, None] == shards[None, :]).astype(jnp.int32)
    ranks = lax.optimization_barrier(jnp.sum((jnp.cumsum(onehot, axis=0) - 1) * onehot, axis=1))
    return ((group_routes * CAP + ranks).astype(jnp.int32), lax.optimization_barrier(jnp.sum(onehot, axis=0)).astype(jnp.int32))

def pick_rows(table, indices):
    return jnp.take(table, indices, axis=0)

def reference(hidden, connector, routing, talker_in, norm_gain, kv_weight, kv_grad):
    group_routes = routing[:, 0].reshape(N_DP, TOK_DEV)
    slot_ids, counts = jax.vmap(slot_index)(group_routes)
    usable = (jnp.arange(CAP, dtype=jnp.int32)[None, None, :] < counts[:, :, None]).reshape(SLOTS)
    masked = jnp.where(usable[:, None], kv_grad, jnp.zeros_like(kv_grad))
    inputs = talker_in.astype(jnp.float32)
    inv_rms = lax.rsqrt(lax.optimization_barrier(jnp.mean(inputs * inputs, axis=1, keepdims=True)) + 1e-06)
    scaled = inputs * inv_rms
    normed = (scaled * norm_gain).astype(jnp.bfloat16)
    factor = 1.0 / math.sqrt(TOKENS)
    kv_weight_grad = jnp.dot(normed.T, masked, preferred_element_type=jnp.float32) * factor
    back_grad = jnp.dot(masked, kv_weight.T, preferred_element_type=jnp.float32)
    gain_back = norm_gain * back_grad
    talker_grad = (inv_rms * (gain_back - scaled * lax.optimization_barrier(jnp.mean(gain_back * scaled, axis=1, keepdims=True)))).astype(jnp.bfloat16)
    grouped = talker_grad.reshape(N_DP, N_TENSOR * CAP, DT)
    row_grad = jax.vmap(pick_rows)(grouped, slot_ids).reshape(TOKENS, DT)
    hidden_grad = jnp.dot(row_grad, connector.T, preferred_element_type=jnp.float32).astype(jnp.bfloat16)
    connector_grad = jnp.dot(hidden.T, row_grad, preferred_element_type=jnp.float32) * factor
    return (hidden_grad, connector_grad, kv_weight_grad)
```

```python
import math

import jax
import jax.numpy as jnp
from jax import lax
from jax.sharding import PartitionSpec as P

CONTRACT_LAST = (((1,), (1,)), ((), ()))
CONTRACT_FIRST = (((0,), (0,)), ((), ()))
ROWS_BY_COLS = (((1,), (0,)), ((), ()))
CHUNKS = 4
F32 = jnp.float32
BF16 = jnp.bfloat16


def dot(a, b, dims):
    return lax.dot_general(a, b, dims, preferred_element_type=F32)


def strides_of(count):
    found = []
    step = count // 2
    while step:
        found.append(step)
        step //= 2
    return found


def bit_reverse(index, count):
    out = jnp.zeros_like(index)
    for place, step in enumerate(strides_of(count)):
        out = out + ((index // step) % 2) * (1 << place)
    return out


def on_device(hidden, connector, routing, talker_in, norm_gain, kv_weight, kv_grad):
    dp_count = lax.axis_size("dp")
    tensor_count = lax.axis_size("tensor")
    pair = 2 if dp_count % 2 == 0 else 1
    line = dp_count // pair
    rows_dev, width = hidden.shape
    capacity, features = talker_in.shape
    kv_cols = kv_grad.shape[1]
    factor = 1.0 / math.sqrt(rows_dev * dp_count)
    dp_pos = lax.axis_index("dp")
    tensor_pos = lax.axis_index("tensor")
    line_pos, pair_pos = dp_pos // pair, dp_pos % pair
    steps = strides_of(tensor_count)

    def tensor_swap(array, step):
        return lax.ppermute(array, "tensor", [(i, i ^ step) for i in range(tensor_count)])

    def pair_swap(array):
        return lax.ppermute(array, "dp", [(i, i ^ 1) for i in range(dp_count)])

    def line_shift(array, by):
        moves = [(i, ((i // pair + by) % line) * pair + i % pair) for i in range(dp_count)]
        return lax.ppermute(array, "dp", moves)

    chunk = width // CHUNKS
    held = []
    for c in range(CHUNKS):
        block = hidden[:, c * chunk:(c + 1) * chunk]
        blocks = [block]
        for _ in range(line - 1):
            block = line_shift(block, 1)
            blocks.append(block)
        held.append(blocks)

    def tensor_blocks(array):
        found = {0: array}
        for step in steps:
            for d in list(found):
                found[d ^ step] = tensor_swap(found[d], step)
        return found

    kv_blocks = tensor_blocks(kv_grad)
    in_blocks = tensor_blocks(talker_in)
    order = sorted(in_blocks)

    route_rows = routing[:, 0]
    earlier = jnp.arange(rows_dev)[None, :] < jnp.arange(rows_dev)[:, None]
    same = route_rows[:, None] == route_rows[None, :]
    ranks = jnp.sum((same & earlier).astype(jnp.int32), axis=1)
    spot = jnp.zeros_like(route_rows)
    for place, d in enumerate(order):
        spot = jnp.where(route_rows == (tensor_pos ^ d), place * capacity + ranks, spot)
    pick = (spot[:, None] == jnp.arange(tensor_count * capacity)[None, :]).astype(BF16)

    kv_all = jnp.concatenate([kv_blocks[d] for d in order], axis=0)
    in_all = jnp.concatenate([in_blocks[d] for d in order], axis=0)
    masked = dot(pick, kv_all, ROWS_BY_COLS).astype(BF16)
    inputs = dot(pick, in_all, ROWS_BY_COLS)

    inv_rms = lax.rsqrt(jnp.mean(inputs * inputs, axis=1, keepdims=True) + 1e-06)
    scaled = inputs * inv_rms
    normed = (scaled * norm_gain).astype(BF16)
    gain_back = norm_gain * dot(masked, kv_weight, CONTRACT_LAST)
    row_grad = (
        inv_rms * (gain_back - scaled * jnp.mean(gain_back * scaled, axis=1, keepdims=True))
    ).astype(BF16)

    share = rows_dev // tensor_count
    cols = features // dp_count
    mine = lax.dynamic_slice_in_dim(row_grad, bit_reverse(tensor_pos, tensor_count) * share, share, 0)
    mine = mine.reshape(share, dp_count, cols).transpose(1, 0, 2)
    got = []
    for s in range(line):
        target = ((line_pos + s) % line) * pair
        piece = jnp.stack([
            lax.dynamic_index_in_dim(mine, target + (pair_pos + o) % pair, 0, keepdims=False)
            for o in range(pair)
        ])
        got.append(line_shift(piece, s) if s else piece)
    shared = jnp.stack(got, axis=1)
    for step in steps:
        other = tensor_swap(shared, step)
        low = (tensor_pos // step) % 2 == 0
        shared = jnp.where(
            low,
            jnp.concatenate([shared, other], axis=2),
            jnp.concatenate([other, shared], axis=2),
        )
    sides = shared.reshape(pair, line * rows_dev, cols)

    per_dev = kv_cols // (dp_count * tensor_count)
    masked_t = masked.T.reshape(dp_count, tensor_count, per_dev, rows_dev)
    masked_t = lax.dynamic_index_in_dim(masked_t, tensor_pos, 1, keepdims=False)
    terms = dot(masked_t.reshape(dp_count * per_dev, rows_dev), normed, ROWS_BY_COLS) * factor
    terms = terms.reshape(line, pair, per_dev, features)
    own_terms = lax.dynamic_index_in_dim(terms, pair_pos, 1, keepdims=False)
    if pair == 2:
        far_terms = lax.dynamic_index_in_dim(terms, 1 - pair_pos, 1, keepdims=False)
        own_terms = own_terms + pair_swap(far_terms.astype(BF16)).astype(F32)
    kv_out = lax.dynamic_index_in_dim(own_terms, line_pos, 0, keepdims=False)
    for s in range(1, line):
        piece = lax.dynamic_index_in_dim(own_terms, (line_pos + s) % line, 0, keepdims=False)
        kv_out = kv_out + line_shift(piece.astype(BF16), s).astype(F32)
    kv_weight_grad = kv_out.T

    hidden_grad = dot(row_grad, connector, CONTRACT_LAST).astype(BF16)

    outs = []
    for blocks in held:
        rows = jnp.concatenate(blocks, axis=0)
        total = dot(rows, sides[0], CONTRACT_FIRST) * factor
        if pair == 2:
            far = (dot(rows, sides[1], CONTRACT_FIRST) * factor).astype(BF16)
            total = total + pair_swap(far).astype(F32)
        outs.append(total)
    connector_grad = jnp.concatenate(outs, axis=0)
    return (hidden_grad, connector_grad, kv_weight_grad)


def solution(mesh):
    return jax.shard_map(
        on_device,
        mesh=mesh,
        in_specs=(
            P("dp", "tensor"),
            P("tensor", None),
            P("dp", None),
            P(("dp", "tensor"), None),
            P(),
            P(),
            P(("dp", "tensor"), None),
        ),
        out_specs=(P("dp", "tensor"), P("tensor", "dp"), P(None, ("dp", "tensor"))),
        check_vma=False,
    )
```

```python
import math

import jax
import jax.numpy as jnp
from jax import lax
from jax.sharding import PartitionSpec as P

CONTRACT_LAST = (((1,), (1,)), ((), ()))
ROWS_BY_COLS = (((1,), (0,)), ((), ()))
COLS_BY_LAST = (((0,), (1,)), ((), ()))
PARTS = 4
F32 = jnp.float32
BF16 = jnp.bfloat16


def dot(a, b, dims):
    return lax.dot_general(a, b, dims, preferred_element_type=F32)


def strides_of(count):
    found = []
    step = count // 2
    while step:
        found.append(step)
        step //= 2
    return found


def at(array, index, axis=0):
    return lax.dynamic_index_in_dim(array, index, axis, keepdims=False)


def on_device(hidden, connector, routing, talker_in, norm_gain, kv_weight, kv_grad):
    dp_count = lax.axis_size("dp")
    tensor_count = lax.axis_size("tensor")
    pair = 2
    line = dp_count // pair
    rows_dev, width = hidden.shape
    capacity, features = talker_in.shape
    kv_cols = kv_grad.shape[1]
    cols = features // dp_count
    share = cols // tensor_count
    factor = 1.0 / math.sqrt(rows_dev * dp_count)
    dp_pos = lax.axis_index("dp")
    tensor_pos = lax.axis_index("tensor")
    line_pos, pair_pos = dp_pos // pair, dp_pos % pair
    lines = [[i * pair + j for i in range(line)] for j in range(pair)]
    steps = strides_of(tensor_count)

    def tensor_swap(array, step):
        return lax.ppermute(array, "tensor", [(i, i ^ step) for i in range(tensor_count)])

    def pair_swap(array):
        return lax.ppermute(array, "dp", [(i, i ^ 1) for i in range(dp_count)])

    def line_shift(array, by):
        moves = [(i, ((i // pair + by) % line) * pair + i % pair) for i in range(dp_count)]
        return lax.ppermute(array, "dp", moves)

    def digit(step):
        return (tensor_pos // step) % 2

    def tensor_blocks(array, some):
        for step in some:
            array = jnp.concatenate([array, tensor_swap(array, step)], axis=-1)
        return array

    def tensor_split(array, some):
        for step in some:
            own, other = at(array, digit(step), array.ndim - 3), at(array, 1 - digit(step), array.ndim - 3)
            array = jnp.concatenate([own, tensor_swap(other, step)], axis=-1)
        return array

    def tensor_gather(array, axis, some):
        for step in some:
            other = tensor_swap(array, step)
            array = jnp.where(
                digit(step) == 0,
                jnp.stack([array, other], axis=axis),
                jnp.stack([other, array], axis=axis),
            )
        return array

    def line_exchange(blocks):
        return lax.all_to_all(
            blocks, "dp", split_axis=0, concat_axis=0, tiled=True, axis_index_groups=lines
        )

    together = lax.optimization_barrier
    far_step, near_steps = steps[:1], steps[1:]
    twos = (2,) * len(steps)

    held = lax.all_gather(hidden, "dp", axis=0, tiled=True, axis_index_groups=lines)

    routes = routing[:, 0]
    row_ids = jnp.arange(rows_dev)
    same = routes[:, None] == routes[None, :]
    ranks = jnp.sum((same & (row_ids[None, :] < row_ids[:, None])).astype(jnp.int32), axis=1)
    distance = routes ^ tensor_pos
    place = jnp.zeros_like(routes)
    for k, step in enumerate(steps):
        place = place + ((distance // step) % 2) * (1 << k)
    spot = place * capacity + ranks
    pick = (spot[:, None] == jnp.arange(tensor_count * capacity)[None, :]).astype(BF16)

    inputs = talker_in.T.astype(F32)
    inv_rms = lax.rsqrt(jnp.mean(inputs * inputs, axis=0, keepdims=True) + 1e-06)
    scaled = inputs * inv_rms
    gain = norm_gain[:, None]
    gain_back = gain * dot(kv_weight, kv_grad, CONTRACT_LAST)
    grad = (
        inv_rms * (gain_back - scaled * jnp.mean(gain_back * scaled, axis=0, keepdims=True))
    ).astype(BF16)
    normed = (scaled * gain).astype(BF16).reshape(twos + (features // tensor_count, capacity))

    shares = tensor_split(grad.reshape((dp_count,) + twos + (share, capacity)), far_step)
    shares = tensor_split(shares, near_steps)
    rows = dot(shares.reshape(dp_count * share, -1), pick, CONTRACT_LAST).astype(BF16)
    rows, normed, kv_t = together((rows.reshape(dp_count, share, rows_dev), normed, kv_grad.T))
    normed = tensor_split(normed, far_step)
    kv_slots = tensor_blocks(kv_t, far_step)

    sided = rows.reshape(line, 2, share, rows_dev)
    sided = jnp.where(pair_pos == 0, sided, sided[:, ::-1])
    got = [at(sided, line_pos)]
    got += [line_shift(at(sided, (line_pos + s) % line), s) for s in range(1, line)]
    normed = dot(tensor_split(normed, near_steps), pick, CONTRACT_LAST).astype(BF16)
    masked = dot(tensor_blocks(kv_slots, near_steps), pick, CONTRACT_LAST).astype(BF16)
    per_dev = kv_cols // (dp_count * tensor_count)
    block = kv_cols // dp_count
    masked = masked.reshape(line, 2, block, rows_dev)
    own = at(masked, pair_pos, 1).reshape(line * block, rows_dev)
    other = at(masked, 1 - pair_pos, 1).reshape(line * block, rows_dev)
    row_grad = tensor_gather(rows, 1, far_step)
    got, row_grad, own, normed, sent = together(
        (got, row_grad, own, normed, jnp.concatenate([other, normed], axis=0))
    )
    origin = (line_pos - jnp.arange(line)) % line
    got = jnp.take(jnp.stack(got), origin, axis=0)
    got = got.transpose(1, 2, 0, 3).reshape(2, share, line * rows_dev)
    got = tensor_gather(got, 1, far_step)
    far = pair_swap(sent)
    grads = tensor_gather(got, 1, near_steps).reshape(2, cols, line * rows_dev)
    row_grad = tensor_gather(row_grad, 1, near_steps).reshape(features, rows_dev)
    terms = dot(own, normed, CONTRACT_LAST)
    terms = terms + dot(far[:line * block], far[line * block:], CONTRACT_LAST)
    terms = (terms * factor).reshape(line, block, -1)
    held, grads, row_grad, terms = together((held, grads, row_grad, terms))

    part = width // PARTS
    held = [held[:, c * part:(c + 1) * part] for c in range(PARTS)]
    fars = [(dot(grads[1], rows, ROWS_BY_COLS) * factor).astype(BF16) for rows in held]
    gots = [pair_swap(far) for far in fars]
    terms, row_grad, fars[-1] = together((terms, row_grad, fars[-1]))
    hidden_grad = dot(row_grad, connector, COLS_BY_LAST).astype(BF16)
    kv_out = at(terms, line_pos)
    for s in range(1, line):
        kv_out = kv_out + line_shift(at(terms, (line_pos + s) % line).astype(BF16), s).astype(F32)
    kv_out = kv_out.reshape(twos + (per_dev, -1))
    for k, step in enumerate(steps):
        own, other = at(kv_out, digit(step)), at(kv_out, 1 - digit(step))
        other = tensor_swap(other, step)
        spot = len(steps) - k
        kv_out = jnp.where(
            digit(step) == 0,
            jnp.stack([own, other], axis=spot),
            jnp.stack([other, own], axis=spot),
        )
    kv_weight_grad = kv_out.reshape(per_dev, features).T
    gots[1], hidden_grad = together((gots[1], hidden_grad))
    outs = [
        dot(rows, grads[0], COLS_BY_LAST) * factor + got.T.astype(F32)
        for rows, got in zip(held, gots)
    ]
    connector_grad = jnp.concatenate(outs, axis=0)
    return (hidden_grad, connector_grad, kv_weight_grad)


def solution(mesh):
    return jax.shard_map(
        on_device,
        mesh=mesh,
        in_specs=(
            P("dp", "tensor"),
            P("tensor", None),
            P("dp", None),
            P(("dp", "tensor"), None),
            P(),
            P(),
            P(("dp", "tensor"), None),
        ),
        out_specs=(P("dp", "tensor"), P("tensor", "dp"), P(None, ("dp", "tensor"))),
        check_vma=False,
    )
```

```python
import math

import jax
import jax.numpy as jnp
from jax import lax
from jax.sharding import PartitionSpec as P

CONTRACT_LAST = (((1,), (1,)), ((), ()))
ROWS_BY_COLS = (((1,), (0,)), ((), ()))
COLS_BY_LAST = (((0,), (1,)), ((), ()))
PARTS = 4
F32 = jnp.float32
BF16 = jnp.bfloat16


def dot(a, b, dims):
    return lax.dot_general(a, b, dims, preferred_element_type=F32)


def strides_of(count):
    found = []
    step = count // 2
    while step:
        found.append(step)
        step //= 2
    return found


def at(array, index, axis=0):
    return lax.dynamic_index_in_dim(array, index, axis, keepdims=False)


def on_device(hidden, connector, routing, talker_in, norm_gain, kv_weight, kv_grad):
    dp_count = lax.axis_size("dp")
    tensor_count = lax.axis_size("tensor")
    pair = 2
    line = dp_count // pair
    rows_dev, width = hidden.shape
    capacity, features = talker_in.shape
    kv_cols = kv_grad.shape[1]
    cols = features // dp_count
    share = cols // tensor_count
    factor = 1.0 / math.sqrt(rows_dev * dp_count)
    dp_pos = lax.axis_index("dp")
    tensor_pos = lax.axis_index("tensor")
    line_pos, pair_pos = dp_pos // pair, dp_pos % pair
    lines = [[i * pair + j for i in range(line)] for j in range(pair)]
    steps = strides_of(tensor_count)

    def tensor_swap(array, step):
        return lax.ppermute(array, "tensor", [(i, i ^ step) for i in range(tensor_count)])

    def pair_swap(array):
        return lax.ppermute(array, "dp", [(i, i ^ 1) for i in range(dp_count)])

    def line_shift(array, by):
        moves = [(i, ((i // pair + by) % line) * pair + i % pair) for i in range(dp_count)]
        return lax.ppermute(array, "dp", moves)

    def digit(step):
        return (tensor_pos // step) % 2

    def tensor_blocks(array, some):
        for step in some:
            array = jnp.concatenate([array, tensor_swap(array, step)], axis=-1)
        return array

    def tensor_split(array, some):
        for step in some:
            own, other = at(array, digit(step), array.ndim - 3), at(array, 1 - digit(step), array.ndim - 3)
            array = jnp.concatenate([own, tensor_swap(other, step)], axis=-1)
        return array

    def tensor_gather(array, axis, some):
        for step in some:
            other = tensor_swap(array, step)
            array = jnp.where(
                digit(step) == 0,
                jnp.stack([array, other], axis=axis),
                jnp.stack([other, array], axis=axis),
            )
        return array

    def line_exchange(blocks):
        return lax.all_to_all(
            blocks, "dp", split_axis=0, concat_axis=0, tiled=True, axis_index_groups=lines
        )

    together = lax.optimization_barrier
    far_step, near_steps = steps[:1], steps[1:]
    twos = (2,) * len(steps)

    held = lax.all_gather(hidden, "dp", axis=0, tiled=True, axis_index_groups=lines)

    routes = routing[:, 0]
    row_ids = jnp.arange(rows_dev)
    same = routes[:, None] == routes[None, :]
    ranks = jnp.sum((same & (row_ids[None, :] < row_ids[:, None])).astype(jnp.int32), axis=1)
    distance = routes ^ tensor_pos
    place = jnp.zeros_like(routes)
    for k, step in enumerate(steps):
        place = place + ((distance // step) % 2) * (1 << k)
    spot = place * capacity + ranks
    pick = (spot[:, None] == jnp.arange(tensor_count * capacity)[None, :]).astype(BF16)

    inputs = talker_in.T.astype(F32)
    inv_rms = lax.rsqrt(jnp.mean(inputs * inputs, axis=0, keepdims=True) + 1e-06)
    scaled = inputs * inv_rms
    gain = norm_gain[:, None]
    gain_back = gain * dot(kv_weight, kv_grad, CONTRACT_LAST)
    grad = (
        inv_rms * (gain_back - scaled * jnp.mean(gain_back * scaled, axis=0, keepdims=True))
    ).astype(BF16)
    normed = (scaled * gain).astype(BF16).reshape(twos + (features // tensor_count, capacity))

    shares = tensor_split(grad.reshape((dp_count,) + twos + (share, capacity)), far_step)
    shares = tensor_split(shares, near_steps)
    rows = dot(shares.reshape(dp_count * share, -1), pick, CONTRACT_LAST).astype(BF16)
    rows, normed, kv_t = together((rows.reshape(dp_count, share, rows_dev), normed, kv_grad.T))
    normed = tensor_split(normed, far_step)
    kv_slots = tensor_blocks(kv_t, far_step)

    sided = rows.reshape(line, 2, share, rows_dev)
    sided = jnp.where(pair_pos == 0, sided, sided[:, ::-1])
    got = [at(sided, line_pos)]
    got += [line_shift(at(sided, (line_pos + s) % line), s) for s in range(1, line)]
    normed = dot(tensor_split(normed, near_steps), pick, CONTRACT_LAST).astype(BF16)
    masked = dot(tensor_blocks(kv_slots, near_steps), pick, CONTRACT_LAST).astype(BF16)
    per_dev = kv_cols // (dp_count * tensor_count)
    block = kv_cols // dp_count
    masked = masked.reshape(line, 2, block, rows_dev)
    own = at(masked, pair_pos, 1).reshape(line * block, rows_dev)
    other = at(masked, 1 - pair_pos, 1).reshape(line * block, rows_dev)
    row_grad = tensor_gather(rows, 1, far_step)
    got, row_grad, own, normed, sent = together(
        (got, row_grad, own, normed, jnp.concatenate([other, normed], axis=0))
    )
    origin = (line_pos - jnp.arange(line)) % line
    got = jnp.take(jnp.stack(got), origin, axis=0)
    got = got.transpose(1, 2, 0, 3).reshape(2, share, line * rows_dev)
    got = tensor_gather(got, 1, far_step)
    far = pair_swap(sent)
    grads = tensor_gather(got, 1, near_steps).reshape(2, cols, line * rows_dev)
    row_grad = tensor_gather(row_grad, 1, near_steps).reshape(features, rows_dev)
    terms = dot(own, normed, CONTRACT_LAST)
    terms = terms + dot(far[:line * block], far[line * block:], CONTRACT_LAST)
    terms = (terms * factor).reshape(line, block, -1)
    held, grads, row_grad, terms = together((held, grads, row_grad, terms))

    part = width // PARTS
    gots, blocks = [], []
    for c in range(PARTS):
        if c > 1:
            gots[c - 2], held = together((gots[c - 2], held))
        blocks.append(held[:, c * part:(c + 1) * part])
        far_c = (dot(grads[1], blocks[c], ROWS_BY_COLS) * factor).astype(BF16)
        if c == 2:
            far_c, row_grad = together((far_c, row_grad))
        gots.append(pair_swap(far_c))
    hidden_grad = dot(row_grad, connector, COLS_BY_LAST).astype(BF16)
    gots[0], terms = together((gots[0], terms))
    kv_out = at(terms, line_pos)
    for s in range(1, line):
        kv_out = kv_out + line_shift(at(terms, (line_pos + s) % line).astype(BF16), s).astype(F32)
    kv_out = kv_out.reshape(twos + (per_dev, -1))
    for k, step in enumerate(steps):
        own, other = at(kv_out, digit(step)), at(kv_out, 1 - digit(step))
        other = tensor_swap(other, step)
        spot = len(steps) - k
        kv_out = jnp.where(
            digit(step) == 0,
            jnp.stack([own, other], axis=spot),
            jnp.stack([other, own], axis=spot),
        )
    kv_weight_grad = kv_out.reshape(per_dev, features).T
    gots[2], hidden_grad = together((gots[2], hidden_grad))
    outs = [
        dot(rows, grads[0], COLS_BY_LAST) * factor + got.T.astype(F32)
        for rows, got in zip(blocks, gots)
    ]
    connector_grad = jnp.concatenate(outs, axis=0)
    return (hidden_grad, connector_grad, kv_weight_grad)


def solution(mesh):
    return jax.shard_map(
        on_device,
        mesh=mesh,
        in_specs=(
            P("dp", "tensor"),
            P("tensor", None),
            P("dp", None),
            P(("dp", "tensor"), None),
            P(),
            P(),
            P(("dp", "tensor"), None),
        ),
        out_specs=(P("dp", "tensor"), P("tensor", "dp"), P(None, ("dp", "tensor"))),
        check_vma=False,
    )
```

```python
import math

import jax
import jax.numpy as jnp
from jax import lax
from jax.sharding import PartitionSpec as P

CONTRACT_LAST = (((1,), (1,)), ((), ()))
ROWS_BY_COLS = (((1,), (0,)), ((), ()))
COLS_BY_LAST = (((0,), (1,)), ((), ()))
PARTS = 4
EARLY = 2
F32 = jnp.float32
BF16 = jnp.bfloat16


def dot(a, b, dims):
    return lax.dot_general(a, b, dims, preferred_element_type=F32)


def strides_of(count):
    found = []
    step = count // 2
    while step:
        found.append(step)
        step //= 2
    return found


def at(array, index, axis=0):
    return lax.dynamic_index_in_dim(array, index, axis, keepdims=False)


def on_device(hidden, connector, routing, talker_in, norm_gain, kv_weight, kv_grad):
    dp_count = lax.axis_size("dp")
    tensor_count = lax.axis_size("tensor")
    pair = 2
    line = dp_count // pair
    rows_dev, width = hidden.shape
    capacity, features = talker_in.shape
    kv_cols = kv_grad.shape[1]
    cols = features // dp_count
    share = cols // tensor_count
    factor = 1.0 / math.sqrt(rows_dev * dp_count)
    dp_pos = lax.axis_index("dp")
    tensor_pos = lax.axis_index("tensor")
    line_pos, pair_pos = dp_pos // pair, dp_pos % pair
    lines = [[i * pair + j for i in range(line)] for j in range(pair)]
    steps = strides_of(tensor_count)

    def tensor_swap(array, step):
        return lax.ppermute(array, "tensor", [(i, i ^ step) for i in range(tensor_count)])

    def pair_swap(array):
        return lax.ppermute(array, "dp", [(i, i ^ 1) for i in range(dp_count)])

    def line_swap(array, by):
        moves = [(i, (i // pair ^ by) * pair + i % pair) for i in range(dp_count)]
        return lax.ppermute(array, "dp", moves)

    def digit(step):
        return (tensor_pos // step) % 2

    def tensor_blocks(array, some):
        for step in some:
            array = jnp.concatenate([array, tensor_swap(array, step)], axis=-1)
        return array

    def tensor_split(array, some):
        for step in some:
            own, other = at(array, digit(step), array.ndim - 3), at(array, 1 - digit(step), array.ndim - 3)
            array = jnp.concatenate([own, tensor_swap(other, step)], axis=-1)
        return array

    def tensor_gather(array, axis, some):
        for step in some:
            other = tensor_swap(array, step)
            array = jnp.where(
                digit(step) == 0,
                jnp.stack([array, other], axis=axis),
                jnp.stack([other, array], axis=axis),
            )
        return array

    together = lax.optimization_barrier
    far_step, near_steps = steps[:1], steps[1:]
    twos = (2,) * len(steps)

    part = width // PARTS
    spread = [{0: hidden[:, c * part:(c + 1) * part]} for c in range(PARTS)]

    def hop(c, bits):
        for d in range(line):
            if bin(d).count("1") == bits:
                low = d & -d
                spread[c][d] = line_swap(spread[c][d - low], low)

    hop(0, 1)

    routes = routing[:, 0]
    row_ids = jnp.arange(rows_dev)
    same = routes[:, None] == routes[None, :]
    ranks = jnp.sum((same & (row_ids[None, :] < row_ids[:, None])).astype(jnp.int32), axis=1)
    distance = routes ^ tensor_pos
    place = jnp.zeros_like(routes)
    for k, step in enumerate(steps):
        place = place + ((distance // step) % 2) * (1 << k)
    spot = place * capacity + ranks
    pick = (spot[:, None] == jnp.arange(tensor_count * capacity)[None, :]).astype(BF16)

    inputs = talker_in.T.astype(F32)
    inv_rms = lax.rsqrt(jnp.mean(inputs * inputs, axis=0, keepdims=True) + 1e-06)
    scaled = inputs * inv_rms
    gain = norm_gain[:, None]
    gain_back = gain * dot(kv_weight, kv_grad, CONTRACT_LAST)
    grad = (
        inv_rms * (gain_back - scaled * jnp.mean(gain_back * scaled, axis=0, keepdims=True))
    ).astype(BF16)
    normed = (scaled * gain).astype(BF16).reshape(twos + (features // tensor_count, capacity))

    grad, spread = together((grad, spread))
    hop(1, 1)
    shares = tensor_split(grad.reshape((dp_count,) + twos + (share, capacity)), far_step)
    shares, spread = together((shares, spread))
    hop(0, 2)
    hop(1, 2)
    shares = tensor_split(shares, near_steps)
    rows = dot(shares.reshape(dp_count * share, -1), pick, CONTRACT_LAST).astype(BF16)
    rows = rows.reshape(dp_count, share, rows_dev)
    rows, normed, kv_t = together((rows, normed, kv_grad.T))

    sided = rows.reshape(line, 2, share, rows_dev)
    sided = jnp.where(pair_pos == 0, sided, sided[:, ::-1])
    got = lax.all_to_all(
        sided, "dp", split_axis=0, concat_axis=0, tiled=True, axis_index_groups=lines
    )
    normed = tensor_split(normed, far_step)
    kv_slots = tensor_blocks(kv_t, far_step)
    got, normed, kv_slots, spread = together((got, normed, kv_slots, spread))
    hop(2, 1)
    got = jnp.take(got, line_pos ^ jnp.arange(line), axis=0).transpose(1, 2, 0, 3).reshape(2, share, line * rows_dev)
    got = tensor_gather(got, 1, far_step)
    normed = dot(tensor_split(normed, near_steps), pick, CONTRACT_LAST).astype(BF16)
    masked = dot(tensor_blocks(kv_slots, near_steps), pick, CONTRACT_LAST).astype(BF16)
    per_dev = kv_cols // (dp_count * tensor_count)
    block = kv_cols // dp_count
    masked = masked.reshape(line, 2, block, rows_dev)
    own = at(masked, pair_pos, 1).reshape(line * block, rows_dev)
    other = at(masked, 1 - pair_pos, 1).reshape(line * block, rows_dev)
    sent = jnp.concatenate([other, normed], axis=0)
    got, rows, own, normed, sent, spread = together((got, rows, own, normed, sent, spread))
    hop(2, 2)
    hop(3, 1)
    for bits in range(3, line.bit_length()):
        for c in range(EARLY):
            hop(c, bits)
    far = pair_swap(sent)
    grads = tensor_gather(got, 1, near_steps).reshape(2, cols, line * rows_dev)

    def terms_of(c):
        rows = jnp.concatenate([spread[c][d] for d in range(line)], axis=0)
        return rows, (dot(grads[1], rows, ROWS_BY_COLS) * factor).astype(BF16)

    pairs = [terms_of(c) for c in range(EARLY)]
    held, fars = [p[0] for p in pairs], [p[1] for p in pairs]
    fars, spread = together((fars, spread))
    gots = [pair_swap(far_c) for far_c in fars]
    hop(3, 2)
    for bits in range(3, line.bit_length()):
        for c in range(EARLY, PARTS):
            hop(c, bits)
    row_grad = tensor_gather(rows, 1, steps).reshape(features, rows_dev)
    row_grad, fars = together((row_grad, fars))
    hidden_grad = dot(row_grad, connector, COLS_BY_LAST).astype(BF16)
    gots[0], spread, hidden_grad = together((gots[0], spread, hidden_grad))
    pairs = [terms_of(c) for c in range(EARLY, PARTS)]
    held += [p[0] for p in pairs]
    gots += [pair_swap(p[1]) for p in pairs]
    gots[0], own, far = together((gots[0], own, far))
    terms = dot(own, normed, CONTRACT_LAST)
    terms = terms + dot(far[:line * block], far[line * block:], CONTRACT_LAST)
    terms = (terms * factor).reshape(line, block, -1)
    kv_out = at(terms, line_pos)
    for d in range(1, line):
        kv_out = kv_out + line_swap(at(terms, line_pos ^ d).astype(BF16), d).astype(F32)
    kv_out = kv_out.reshape(twos + (per_dev, -1))
    for k, step in enumerate(steps):
        own, other = at(kv_out, digit(step)), at(kv_out, 1 - digit(step))
        other = tensor_swap(other, step)
        spot = len(steps) - k
        kv_out = jnp.where(
            digit(step) == 0,
            jnp.stack([own, other], axis=spot),
            jnp.stack([other, own], axis=spot),
        )
    kv_weight_grad = kv_out.reshape(per_dev, features).T
    outs = [
        dot(rows, grads[0], COLS_BY_LAST) * factor + got.T.astype(F32)
        for rows, got in zip(held, gots)
    ]
    connector_grad = jnp.concatenate(outs, axis=0)
    return (hidden_grad, connector_grad, kv_weight_grad)


def solution(mesh):
    return jax.shard_map(
        on_device,
        mesh=mesh,
        in_specs=(
            P("dp", "tensor"),
            P("tensor", None),
            P("dp", None),
            P(("dp", "tensor"), None),
            P(),
            P(),
            P(("dp", "tensor"), None),
        ),
        out_specs=(P("dp", "tensor"), P("tensor", "dp"), P(None, ("dp", "tensor"))),
        check_vma=False,
    )
```

```python
import math

import jax
import jax.numpy as jnp
from jax import lax
from jax.sharding import PartitionSpec as P

CONTRACT_LAST = (((1,), (1,)), ((), ()))
ROWS_BY_COLS = (((1,), (0,)), ((), ()))
COLS_BY_LAST = (((0,), (1,)), ((), ()))
PARTS = 4
EARLY = 2
F32 = jnp.float32
BF16 = jnp.bfloat16


def dot(a, b, dims):
    return lax.dot_general(a, b, dims, preferred_element_type=F32)


def strides_of(count):
    found = []
    step = count // 2
    while step:
        found.append(step)
        step //= 2
    return found


def at(array, index, axis=0):
    return lax.dynamic_index_in_dim(array, index, axis, keepdims=False)


def on_device(hidden, connector, routing, talker_in, norm_gain, kv_weight, kv_grad):
    dp_count = lax.axis_size("dp")
    tensor_count = lax.axis_size("tensor")
    pair = 2
    line = dp_count // pair
    rows_dev, width = hidden.shape
    capacity, features = talker_in.shape
    kv_cols = kv_grad.shape[1]
    cols = features // dp_count
    share = cols // tensor_count
    factor = 1.0 / math.sqrt(rows_dev * dp_count)
    dp_pos = lax.axis_index("dp")
    tensor_pos = lax.axis_index("tensor")
    line_pos, pair_pos = dp_pos // pair, dp_pos % pair
    lines = [[i * pair + j for i in range(line)] for j in range(pair)]
    steps = strides_of(tensor_count)

    def tensor_swap(array, step):
        return lax.ppermute(array, "tensor", [(i, i ^ step) for i in range(tensor_count)])

    def pair_swap(array):
        return lax.ppermute(array, "dp", [(i, i ^ 1) for i in range(dp_count)])

    def line_swap(array, by):
        moves = [(i, (i // pair ^ by) * pair + i % pair) for i in range(dp_count)]
        return lax.ppermute(array, "dp", moves)

    def digit(step):
        return (tensor_pos // step) % 2

    def tensor_blocks(array, some):
        for step in some:
            array = jnp.concatenate([array, tensor_swap(array, step)], axis=-1)
        return array

    def tensor_split(array, some):
        for step in some:
            own, other = at(array, digit(step), array.ndim - 3), at(array, 1 - digit(step), array.ndim - 3)
            array = jnp.concatenate([own, tensor_swap(other, step)], axis=-1)
        return array

    def tensor_gather(array, axis, some):
        for step in some:
            other = tensor_swap(array, step)
            array = jnp.where(
                digit(step) == 0,
                jnp.stack([array, other], axis=axis),
                jnp.stack([other, array], axis=axis),
            )
        return array

    together = lax.optimization_barrier
    far_step, near_steps = steps[:1], steps[1:]
    twos = (2,) * len(steps)

    part = width // PARTS
    spread = [{0: hidden[:, c * part:(c + 1) * part]} for c in range(PARTS)]

    def hop(c, bits):
        for d in range(line):
            if bin(d).count("1") == bits:
                low = d & -d
                spread[c][d] = line_swap(spread[c][d - low], low)

    def joined(c):
        return jnp.concatenate([spread[c][d] for d in range(line)], axis=0)

    hop(0, 1)

    routes = routing[:, 0]
    row_ids = jnp.arange(rows_dev)
    same = routes[:, None] == routes[None, :]
    ranks = jnp.sum((same & (row_ids[None, :] < row_ids[:, None])).astype(jnp.int32), axis=1)
    distance = routes ^ tensor_pos
    place = jnp.zeros_like(routes)
    for k, step in enumerate(steps):
        place = place + ((distance // step) % 2) * (1 << k)
    spot = place * capacity + ranks
    pick = (spot[:, None] == jnp.arange(tensor_count * capacity)[None, :]).astype(BF16)

    inputs = talker_in.T.astype(F32)
    inv_rms = lax.rsqrt(jnp.mean(inputs * inputs, axis=0, keepdims=True) + 1e-06)
    scaled = inputs * inv_rms
    gain = norm_gain[:, None]
    gain_back = gain * dot(kv_weight, kv_grad, CONTRACT_LAST)
    grad = (
        inv_rms * (gain_back - scaled * jnp.mean(gain_back * scaled, axis=0, keepdims=True))
    ).astype(BF16)
    normed = (scaled * gain).astype(BF16).reshape(twos + (features // tensor_count, capacity))

    grad, spread = together((grad, spread))
    hop(1, 1)
    shares = tensor_split(grad.reshape((dp_count,) + twos + (share, capacity)), far_step)
    shares, spread = together((shares, spread))
    hop(0, 2)
    hop(1, 2)
    shares = tensor_split(shares, near_steps)
    rows = dot(shares.reshape(dp_count * share, -1), pick, CONTRACT_LAST).astype(BF16)
    rows = rows.reshape(dp_count, share, rows_dev)
    rows, normed, kv_t = together((rows, normed, kv_grad.T))

    sided = rows.reshape(line, 2, share, rows_dev)
    sided = jnp.where(pair_pos == 0, sided, sided[:, ::-1])
    got = lax.all_to_all(
        sided, "dp", split_axis=0, concat_axis=0, tiled=True, axis_index_groups=lines
    )
    normed = tensor_split(normed, far_step)
    kv_slots = tensor_blocks(kv_t, far_step)
    got, spread = together((got, spread))
    hop(2, 1)
    got = jnp.take(got, line_pos ^ jnp.arange(line), axis=0).transpose(1, 2, 0, 3).reshape(2, share, line * rows_dev)
    got = tensor_gather(got, 1, far_step)
    normed = dot(tensor_split(normed, near_steps), pick, CONTRACT_LAST).astype(BF16)
    masked = dot(tensor_blocks(kv_slots, near_steps), pick, CONTRACT_LAST).astype(BF16)
    per_dev = kv_cols // (dp_count * tensor_count)
    block = kv_cols // dp_count
    masked = masked.reshape(line, 2, block, rows_dev)
    own = at(masked, pair_pos, 1).reshape(line * block, rows_dev)
    other = at(masked, 1 - pair_pos, 1).reshape(line * block, rows_dev)
    sent = jnp.concatenate([other, normed], axis=0)
    early = [joined(c) for c in range(EARLY)] if line == 4 else None
    got, rows, own, normed, sent, spread, early = together(
        (got, rows, own, normed, sent, spread, early)
    )
    hop(2, 2)
    hop(3, 1)
    for bits in range(3, line.bit_length()):
        for c in range(EARLY):
            hop(c, bits)
    far = pair_swap(sent)
    grads = tensor_gather(got, 1, near_steps).reshape(2, cols, line * rows_dev)

    if early is None:
        early = [joined(c) for c in range(EARLY)]

    def terms_of(rows):
        return rows, (dot(grads[1], rows, ROWS_BY_COLS) * factor).astype(BF16)

    pairs = [terms_of(rows_c) for rows_c in early]
    held, fars = [p[0] for p in pairs], [p[1] for p in pairs]
    gots = [pair_swap(far_c) for far_c in fars]
    fars, spread, far = together((fars, spread, far))
    hop(3, 2)
    for bits in range(3, line.bit_length()):
        for c in range(EARLY, PARTS):
            hop(c, bits)
    row_grad = tensor_gather(rows, 1, steps).reshape(features, rows_dev)
    row_grad, fars = together((row_grad, fars))
    hidden_grad = dot(row_grad, connector, COLS_BY_LAST).astype(BF16)
    gots[0], spread, hidden_grad = together((gots[0], spread, hidden_grad))
    pairs = [terms_of(joined(c)) for c in range(EARLY, PARTS)]
    held += [p[0] for p in pairs]
    gots += [pair_swap(p[1]) for p in pairs]
    gots[0], own = together((gots[0], own))
    terms = dot(own, normed, CONTRACT_LAST)
    terms = terms + dot(far[:line * block], far[line * block:], CONTRACT_LAST)
    terms = (terms * factor).reshape(line, block, -1)
    kv_out = at(terms, line_pos)
    for d in range(1, line):
        kv_out = kv_out + line_swap(at(terms, line_pos ^ d).astype(BF16), d).astype(F32)
    kv_out = kv_out.reshape(twos + (per_dev, -1))
    for k, step in enumerate(steps):
        own, other = at(kv_out, digit(step)), at(kv_out, 1 - digit(step))
        other = tensor_swap(other, step)
        spot = len(steps) - k
        kv_out = jnp.where(
            digit(step) == 0,
            jnp.stack([own, other], axis=spot),
            jnp.stack([other, own], axis=spot),
        )
    kv_weight_grad = kv_out.reshape(per_dev, features).T
    outs = [
        dot(rows, grads[0], COLS_BY_LAST) * factor + got.T.astype(F32)
        for rows, got in zip(held, gots)
    ]
    connector_grad = jnp.concatenate(outs, axis=0)
    return (hidden_grad, connector_grad, kv_weight_grad)


def solution(mesh):
    return jax.shard_map(
        on_device,
        mesh=mesh,
        in_specs=(
            P("dp", "tensor"),
            P("tensor", None),
            P("dp", None),
            P(("dp", "tensor"), None),
            P(),
            P(),
            P(("dp", "tensor"), None),
        ),
        out_specs=(P("dp", "tensor"), P("tensor", "dp"), P(None, ("dp", "tensor"))),
        check_vma=False,
    )
```
